32 devices in a mesh: chan: 8 (over y, x, core), tm: 4 (over z).
Axes of the slice: x: 2, y: 2, z: 4, core: 2. Of those that a mesh axis runs over, the one named last changes fastest.
Arguments:
- spectra: bfloat16 [256, 2, 250, 2048], P('tm', None, None, 'chan'), may hold values from -6 to 6
- src_blocks: int32 [2], replicated, may hold values from 0 to 31
- valid: int32 [256], P('tm'), may hold values 0 or 1
Outputs:
- stacked: bfloat16 [128, 101, 2048], P('tm', None, 'chan')
The draws below stay inside these ranges and needn't reach their ends.
All inputs are finite; a program needn't handle non-finite values. No bound on the sum of `valid` on one device may be relied on, other than what follows from the above.
Results may differ from the reference program's by a relative error of at most 0.013.
Values may be sent and summed in bfloat16 or wider, within the bound.
A program may use at most 192 MiB of HBM per device.

```python
import jax
import jax.numpy as jnp
from jax import lax

F = 250
LAGS = 101
SRC_BLK = 64
SEG_DEV = 64
CH = 2048
SEGS = 256
SRC = 128
NBLK = 32
N_TM = 4


def touch_ends(entries, stream_key, smallest, largest):
    shape = entries.shape
    spot = [jax.random.randint(jax.random.fold_in(stream_key, axis), (), 0, shape[axis]) for axis in range(len(shape))]
    entries = entries.at[tuple(spot)].set(smallest)
    longest = shape.index(max(shape))
    spot[longest] = (spot[longest] + 1) % shape[longest]
    return entries.at[tuple(spot)].set(largest)


def steps_of(key, shape, split, smallest, top_value):
    factor_of, own = 1.0, jax.random.fold_in(key, 6)
    for axis_at, parts in split:
        draws = jnp.exp(jax.random.uniform(jax.random.fold_in(own, axis_at), (parts,), jnp.float32, smallest / len(split), top_value / len(split)))
        factor_of = factor_of * jnp.repeat(draws, shape[axis_at] // parts).reshape([-1 if axis == axis_at else 1 for axis in range(len(shape))])
    return factor_of


def noise(rng, shape, width, most, cuts=(), kind=jnp.bfloat16):
    level = steps_of(rng, shape, cuts, -0.22, 0.18) if cuts else 1.0
    entries = jax.random.normal(rng, shape, jnp.float32) * width * level
    return jnp.minimum(jnp.maximum(entries, -most), most).astype(kind)


def setup_inputs(seed: int = 0) -> dict:
    key_of = jax.random.split(jax.random.key(seed), 4)
    spectra = noise(key_of[0], (SEGS, 2, F, CH), 1.0, 6.0, ((0, 4), (3, 8)))
    src_blocks = jax.random.randint(key_of[1], (2,), 0, NBLK).astype(jnp.int32)
    valid = touch_ends((jax.random.randint(key_of[2], (SEGS,), 0, 4) < 3).astype(jnp.int32), jax.random.fold_in(key_of[2], 1), 0, 1)
    return dict(spectra=spectra, src_blocks=src_blocks, valid=valid)


def lag_table(bin_count, lag_count, segment_total):
    bins_idx = jnp.arange(bin_count, dtype=jnp.int32) + 1
    lag_steps = jnp.arange(lag_count, dtype=jnp.int32) - (lag_count - 1) // 2
    phase_int = lag_steps[:, None] * bins_idx[None, :] % (2 * bin_count)
    phase = phase_int.astype(jnp.float32) * (2.0 * jnp.pi / (2.0 * bin_count))
    scale = 1.0 / jnp.sqrt(jnp.float32(segment_total * bin_count))
    return jnp.stack([jnp.cos(phase) * scale, -jnp.sin(phase) * scale]).astype(jnp.bfloat16)

def cross_spectra(source, spectra):
    rotated = jnp.concatenate([spectra[:, 1:2], -spectra[:, 0:1]], axis=1)
    source_wide = source.astype(jnp.float32)
    real_part = jnp.einsum('scfk,scfr->fkr', source_wide, spectra.astype(jnp.float32))
    imag_part = jnp.einsum('scfk,scfr->fkr', source_wide, rotated.astype(jnp.float32))
    return jnp.stack([real_part, imag_part]).astype(jnp.bfloat16)

def to_lags(table, cross):
    result = jnp.einsum('plf,pfkr->klr', table.astype(jnp.float32), cross.astype(jnp.float32))
    return result.astype(jnp.bfloat16)

def reference(spectra, src_blocks, valid):
    table = lag_table(F, LAGS, SEGS)
    grouped = spectra.reshape(N_TM, SEG_DEV, 2, F, CH)
    grouped_mask = valid.reshape(N_TM, SEG_DEV)

    def one_group(carry, inputs):
        shard_spec, shard_mask = inputs
        keep_mask = shard_mask.astype(jnp.bfloat16)[:, None, None, None]
        pieces = []
        for block in range(2):
            start = (src_blocks[block] * SRC_BLK).astype(jnp.int32)
            source = lax.dynamic_slice_in_dim(shard_spec, start, SRC_BLK, 3) * keep_mask
            pieces.append(to_lags(table, cross_spectra(source, shard_spec)))
        partial_value = lax.optimization_barrier(jnp.concatenate(pieces, axis=0))
        return (carry + partial_value.astype(jnp.float32), None)
    start_sum = jnp.zeros((SRC, LAGS, CH), jnp.float32)
    total, _ = lax.scan(one_group, start_sum, (grouped, grouped_mask))
    return total.astype(jnp.bfloat16)
```

```python
import functools

import jax
import jax.numpy as jnp
from jax import lax
from jax.experimental import pallas as pl
from jax.experimental.pallas import tpu as pltpu
from jax.sharding import PartitionSpec as P

LAGS = 101
SRC_BLK = 64
CHUNKS = 4
MIB = 1024 * 1024


def lag_table(bin_count, lag_count, segment_total):
    bins_idx = jnp.arange(bin_count, dtype=jnp.int32) + 1
    lag_steps = jnp.arange(lag_count, dtype=jnp.int32) - (lag_count - 1) // 2
    phase_int = lag_steps[:, None] * bins_idx[None, :] % (2 * bin_count)
    phase = phase_int.astype(jnp.float32) * (2.0 * jnp.pi / (2.0 * bin_count))
    scale = 1.0 / jnp.sqrt(jnp.float32(segment_total * bin_count))
    return jnp.stack([jnp.cos(phase) * scale, -jnp.sin(phase) * scale]).astype(jnp.bfloat16)


def pick_kernel(pick_ref, keep_ref, x_ref, out_ref):
    chunks, bins, rows, depth = out_ref.shape
    for f in range(bins):
        picked = lax.dot_general(
            pick_ref[...], x_ref[f], (((1,), (1,)), ((), ())), preferred_element_type=jnp.float32
        )
        picked = (picked * keep_ref[...]).astype(jnp.bfloat16)
        for j in range(chunks):
            out_ref[j, f] = picked[j * rows:(j + 1) * rows]


def pick_sources(pick, keep, x, bins):
    bin_count, depth, width = x.shape
    rows = pick.shape[0] // CHUNKS
    return pl.pallas_call(
        pick_kernel,
        grid=(bin_count // bins,),
        in_specs=[
            pl.BlockSpec(pick.shape, lambda i: (0, 0)),
            pl.BlockSpec(keep.shape, lambda i: (0, 0)),
            pl.BlockSpec((bins, depth, width), lambda i: (i, 0, 0)),
        ],
        out_specs=pl.BlockSpec((CHUNKS, bins, rows, depth), lambda i: (0, i, 0, 0)),
        out_shape=jax.ShapeDtypeStruct((CHUNKS, bin_count, rows, depth), jnp.bfloat16),
        compiler_params=pltpu.CompilerParams(vmem_limit_bytes=32 * MIB),
        cost_estimate=pl.CostEstimate(
            flops=2 * bin_count * pick.shape[0] * width * depth,
            bytes_accessed=2 * bin_count * depth * (width + pick.shape[0]),
            transcendentals=0,
        ),
    )(pick, keep, x)


def correlate_kernel(stride, bin_count, sign_ref, table_ref, source_ref, x_ref, out_ref, cross):
    bins, rows, depth = source_ref.shape
    width = x_ref.shape[2]
    halves = width // 128
    step = pl.program_id(0)
    sign = sign_ref[...]
    for i in range(bins):
        f = step * bins + i
        real = source_ref[i]
        half = depth // 2
        imag = jnp.concatenate([real[:, half:], real[:, :half]], axis=1) * sign
        both = jnp.concatenate([real, imag], axis=0)
        product = jnp.dot(both, x_ref[i], preferred_element_type=jnp.float32)
        for part in range(2):
            for h in range(halves):
                cross[h, pl.ds(part * bin_count + f, rows, stride=stride), :] = product[
                    part * rows:(part + 1) * rows, h * 128:(h + 1) * 128
                ]

    @pl.when(step == pl.num_programs(0) - 1)
    def _():
        lags = out_ref.shape[1]

        def one_row(k, carry):
            at = pl.multiple_of(k * stride, 8)
            block = jnp.concatenate(
                [cross[h, pl.ds(at, 2 * bin_count), :].astype(jnp.bfloat16) for h in range(halves)], axis=1
            )
            lagged = jnp.dot(table_ref[...], block, preferred_element_type=jnp.float32)
            out_ref[k] = lagged[:lags].astype(jnp.bfloat16)
            return carry

        lax.fori_loop(0, rows, one_row, 0, unroll=4)


def correlate(sign, table, sources, x, chunk, bins):
    _, bin_count, rows, depth = sources.shape
    width = x.shape[2]
    stride = -(-2 * bin_count // 8) * 8
    return pl.pallas_call(
        functools.partial(correlate_kernel, stride, bin_count),
        grid=(bin_count // bins,),
        in_specs=[
            pl.BlockSpec(sign.shape, lambda i: (0, 0)),
            pl.BlockSpec(table.shape, lambda i: (0, 0)),
            pl.BlockSpec((None, bins, rows, depth), lambda i: (chunk, i, 0, 0)),
            pl.BlockSpec((bins, depth, width), lambda i: (i, 0, 0)),
        ],
        out_specs=pl.BlockSpec((rows, LAGS, width), lambda i: (0, 0, 0)),
        out_shape=jax.ShapeDtypeStruct((rows, LAGS, width), jnp.bfloat16),
        scratch_shapes=[pltpu.VMEM((width // 128, rows * stride, 128), jnp.float32)],
        compiler_params=pltpu.CompilerParams(vmem_limit_bytes=48 * MIB),
        cost_estimate=pl.CostEstimate(
            flops=2 * bin_count * 2 * rows * depth * width + 2 * 2 * bin_count * rows * LAGS * width,
            bytes_accessed=2 * bin_count * depth * (width + rows) + 2 * rows * LAGS * width,
            transcendentals=0,
        ),
    )(sign, table, sources, x)


def body(spectra, src_blocks, valid):
    seg_count, _, bin_count, width = spectra.shape
    tm_count = lax.axis_size("tm")
    chan_index = lax.axis_index("chan")
    depth = 2 * seg_count
    sources_all = 2 * SRC_BLK
    per_dev = sources_all // tm_count
    sub = per_dev // CHUNKS

    order = jnp.arange(sources_all, dtype=jnp.int32).reshape(tm_count, CHUNKS, sub)
    order = order.transpose(1, 0, 2).reshape(sources_all)
    channel = src_blocks[order // SRC_BLK] * SRC_BLK + order % SRC_BLK - chan_index * width
    pick = (channel[:, None] == jnp.arange(width, dtype=jnp.int32)[None, :]).astype(jnp.bfloat16)
    keep = jnp.tile(valid.astype(jnp.float32), 2)[None, :]
    sign = jnp.where(jnp.arange(depth) < seg_count, -1.0, 1.0).astype(jnp.bfloat16)[None, :]
    table = lag_table(bin_count, LAGS, seg_count * tm_count)
    table = table.transpose(1, 0, 2).reshape(LAGS, 2 * bin_count)
    table = jnp.pad(table, ((0, -LAGS % 16), (0, 0)))

    x = spectra.transpose(2, 1, 0, 3).reshape(bin_count, depth, width)
    mine = pick_sources(pick, keep, x, 10)
    pieces = []
    for chunk in range(CHUNKS):
        source = lax.psum(mine[chunk], "chan")
        partial_value = correlate(sign, table, source[None], x, 0, 25)
        pieces.append(lax.psum_scatter(partial_value, "tm", scatter_dimension=0, tiled=True))
    return jnp.concatenate(pieces, axis=0)


def solution(mesh):
    placed = (P("tm", None, None, "chan"), P(), P("tm"))
    return jax.shard_map(
        body, mesh=mesh, in_specs=placed, out_specs=P("tm", None, "chan"), check_vma=False
    )
```

```python
import functools

import jax
import jax.numpy as jnp
import ml_dtypes
import numpy as np
from jax import lax
from jax.experimental import pallas as pl
from jax.experimental.pallas import tpu as pltpu
from jax.sharding import PartitionSpec as P

LAGS = 101
SRC_BLK = 64
ROWS = (8, 8, 8, 8)
MIB = 1024 * 1024


def lag_table(bin_count, lag_count, segment_total):
    bins_idx = np.arange(bin_count) + 1
    lag_steps = np.arange(lag_count) - (lag_count - 1) // 2
    phase_int = lag_steps[:, None] * bins_idx[None, :] % (2 * bin_count)
    phase = phase_int * (2.0 * np.pi / (2.0 * bin_count))
    scale = 1.0 / np.sqrt(float(segment_total * bin_count))
    return np.stack([np.cos(phase) * scale, -np.sin(phase) * scale]).astype(ml_dtypes.bfloat16)


def pick_kernel(pick_ref, keep_ref, x_ref, out_ref):
    for f in range(out_ref.shape[0]):
        picked = lax.dot_general(
            pick_ref[...], x_ref[f], (((1,), (1,)), ((), ())), preferred_element_type=jnp.float32
        )
        out_ref[f] = (picked * keep_ref[...]).astype(jnp.bfloat16)


def pick_sources(pick, keep, x, bins):
    bin_count, depth, width = x.shape
    rows = pick.shape[0]
    return pl.pallas_call(
        pick_kernel,
        grid=(bin_count // bins,),
        in_specs=[
            pl.BlockSpec(pick.shape, lambda i: (0, 0)),
            pl.BlockSpec(keep.shape, lambda i: (0, 0)),
            pl.BlockSpec((bins, depth, width), lambda i: (i, 0, 0)),
        ],
        out_specs=pl.BlockSpec((bins, rows, depth), lambda i: (i, 0, 0)),
        out_shape=jax.ShapeDtypeStruct((bin_count, rows, depth), jnp.bfloat16),
        compiler_params=pltpu.CompilerParams(vmem_limit_bytes=32 * MIB),
        cost_estimate=pl.CostEstimate(
            flops=2 * bin_count * rows * width * depth,
            bytes_accessed=2 * bin_count * depth * (width + rows),
            transcendentals=0,
        ),
    )(pick, keep, x)


def correlate_kernel(stride, bin_count, sign_ref, table_ref, source_ref, x_ref, out_ref, cross):
    bins, rows, depth = source_ref.shape
    width = x_ref.shape[2]
    halves = width // 128
    step = pl.program_id(0)
    sign = sign_ref[...]
    for i in range(bins):
        f = step * bins + i
        real = source_ref[i]
        half = depth // 2
        imag = jnp.concatenate([real[:, half:], real[:, :half]], axis=1) * sign
        both = jnp.concatenate([real, imag], axis=0)
        product = jnp.dot(both, x_ref[i], preferred_element_type=jnp.float32)
        for part in range(2):
            for h in range(halves):
                cross[h, pl.ds(part * bin_count + f, rows, stride=stride), :] = product[
                    part * rows:(part + 1) * rows, h * 128:(h + 1) * 128
                ]

    @pl.when(step == pl.num_programs(0) - 1)
    def _():
        lags = out_ref.shape[1]

        def one_row(k, carry):
            at = pl.multiple_of(k * stride, 8)
            block = jnp.concatenate(
                [cross[h, pl.ds(at, 2 * bin_count), :].astype(jnp.bfloat16) for h in range(halves)], axis=1
            )
            lagged = jnp.dot(table_ref[...], block, preferred_element_type=jnp.float32)
            out_ref[k] = lagged[:lags].astype(jnp.bfloat16)
            return carry

        lax.fori_loop(0, rows, one_row, 0, unroll=4)


def correlate(sign, table, sources, x, bins):
    bin_count, rows, depth = sources.shape
    width = x.shape[2]
    stride = -(-2 * bin_count // 8) * 8
    return pl.pallas_call(
        functools.partial(correlate_kernel, stride, bin_count),
        grid=(bin_count // bins,),
        in_specs=[
            pl.BlockSpec(sign.shape, lambda i: (0, 0)),
            pl.BlockSpec(table.shape, lambda i: (0, 0)),
            pl.BlockSpec((bins, rows, depth), lambda i: (i, 0, 0)),
            pl.BlockSpec((bins, depth, width), lambda i: (i, 0, 0)),
        ],
        out_specs=pl.BlockSpec((rows, LAGS, width), lambda i: (0, 0, 0)),
        out_shape=jax.ShapeDtypeStruct((rows, LAGS, width), jnp.bfloat16),
        scratch_shapes=[pltpu.VMEM((width // 128, rows * stride, 128), jnp.float32)],
        compiler_params=pltpu.CompilerParams(vmem_limit_bytes=48 * MIB),
        cost_estimate=pl.CostEstimate(
            flops=2 * bin_count * 2 * rows * depth * width + 2 * 2 * bin_count * rows * LAGS * width,
            bytes_accessed=2 * bin_count * depth * (width + rows) + 2 * rows * LAGS * width,
            transcendentals=0,
        ),
    )(sign, table, sources, x)


def add(a, b):
    return (a.astype(jnp.float32) + b.astype(jnp.float32)).astype(jnp.bfloat16)


def chain_scatter(parts, axis):
    n, at = lax.axis_size(axis), lax.axis_index(axis)
    total = None
    from_left = from_right = None
    for t in range(n - 1):
        to_right = lax.dynamic_index_in_dim(parts, jnp.clip(n - 1 - t + at, 0, n - 1), 0, keepdims=False)
        to_left = lax.dynamic_index_in_dim(parts, jnp.clip(t + at - (n - 1), 0, n - 1), 0, keepdims=False)
        if t:
            to_right, to_left = add(to_right, from_left), add(to_left, from_right)
        from_left = lax.ppermute(to_right, axis, [(i, i + 1) for i in range(t + 1)])
        from_right = lax.ppermute(to_left, axis, [(n - 1 - i, n - 2 - i) for i in range(t + 1)])
    own = lax.dynamic_index_in_dim(parts, at, 0, keepdims=False).astype(jnp.float32)
    total = own + from_left.astype(jnp.float32) + from_right.astype(jnp.float32)
    return total.astype(jnp.bfloat16)


def body(spectra, src_blocks, valid):
    seg_count, _, bin_count, width = spectra.shape
    tm_count = lax.axis_size("tm")
    chan_index = lax.axis_index("chan")
    depth = 2 * seg_count
    sources_all = 2 * SRC_BLK
    per_dev = sources_all // tm_count

    keep = jnp.tile(valid.astype(jnp.float32), 2)[None, :]
    sign = np.where(np.arange(depth) < seg_count, -1.0, 1.0).astype(ml_dtypes.bfloat16)[None, :]
    table = lag_table(bin_count, LAGS, seg_count * tm_count)
    table = table.transpose(1, 0, 2).reshape(LAGS, 2 * bin_count)
    table = np.pad(table, ((0, -LAGS % 16), (0, 0)))
    sign, table = jnp.asarray(sign), jnp.asarray(table)

    def pick_of(first, rows):
        order = np.arange(sources_all, dtype=np.int32).reshape(tm_count, per_dev)
        order = order[:, first:first + rows].reshape(-1)
        channel = src_blocks[order // SRC_BLK] * SRC_BLK + order % SRC_BLK - chan_index * width
        return (channel[:, None] == jnp.arange(width, dtype=jnp.int32)[None, :]).astype(jnp.bfloat16)

    x = spectra.transpose(2, 1, 0, 3).reshape(bin_count, depth, width)
    pieces = []
    source = None
    first = 0
    for rows in ROWS:
        mine = pick_sources(pick_of(first, rows), keep, x, 25)
        if source is not None:
            mine, source = lax.optimization_barrier((mine, source))
        if source is not None:
            pieces.append(source)
        source = lax.psum(mine, "chan")
        first += rows
    pieces.append(source)
    outs = []
    for rows, source in zip(ROWS, pieces):
        partial_value = correlate(sign, table, source, x, 25)
        outs.append(chain_scatter(partial_value.reshape(tm_count, rows, LAGS, width), "tm"))
    return jnp.concatenate(outs, axis=0)


def solution(mesh):
    placed = (P("tm", None, None, "chan"), P(), P("tm"))
    return jax.shard_map(
        body, mesh=mesh, in_specs=placed, out_specs=P("tm", None, "chan"), check_vma=False
    )
```

```python
import functools

import jax
import jax.numpy as jnp
import ml_dtypes
import numpy as np
from jax import lax
from jax.experimental import pallas as pl
from jax.experimental.pallas import tpu as pltpu
from jax.sharding import PartitionSpec as P

LAGS = 101
SRC_BLK = 64
ROWS = (16, 16)
PAD = 256
MIB = 1024 * 1024


def lag_table(bin_count, lag_count, segment_total):
    bins_idx = np.arange(bin_count) + 1
    lag_steps = np.arange(lag_count) - (lag_count - 1) // 2
    phase_int = lag_steps[:, None] * bins_idx[None, :] % (2 * bin_count)
    phase = phase_int * (2.0 * np.pi / (2.0 * bin_count))
    scale = 1.0 / np.sqrt(float(segment_total * bin_count))
    return np.stack([np.cos(phase) * scale, -np.sin(phase) * scale]).astype(ml_dtypes.bfloat16)


def pick_kernel(pick_ref, keep_ref, x_ref, out_ref):
    for f in range(out_ref.shape[0]):
        picked = lax.dot_general(
            pick_ref[...], x_ref[f], (((1,), (1,)), ((), ())), preferred_element_type=jnp.float32
        )
        out_ref[f] = (picked * keep_ref[...]).astype(jnp.bfloat16)


def pick_sources(pick, keep, x, bins):
    bin_count, depth, width = x.shape
    rows = pick.shape[0]
    return pl.pallas_call(
        pick_kernel,
        grid=(bin_count // bins,),
        in_specs=[
            pl.BlockSpec(pick.shape, lambda i: (0, 0)),
            pl.BlockSpec(keep.shape, lambda i: (0, 0)),
            pl.BlockSpec((bins, depth, width), lambda i: (i, 0, 0)),
        ],
        out_specs=pl.BlockSpec((bins, rows, depth), lambda i: (i, 0, 0)),
        out_shape=jax.ShapeDtypeStruct((-(-bin_count // PAD) * PAD, rows, depth), jnp.bfloat16),
        compiler_params=pltpu.CompilerParams(vmem_limit_bytes=32 * MIB),
        cost_estimate=pl.CostEstimate(
            flops=2 * bin_count * rows * width * depth,
            bytes_accessed=2 * bin_count * depth * (width + rows),
            transcendentals=0,
        ),
    )(pick, keep, x)


def correlate_kernel(stride, bin_count, sign_ref, table_ref, source_ref, x_ref, out_ref, cross):
    bins, rows, depth = source_ref.shape
    width = x_ref.shape[2]
    halves = width // 128
    step = pl.program_id(0)
    sign = sign_ref[...]
    for i in range(bins):
        f = step * bins + i
        real = source_ref[i]
        half = depth // 2
        imag = jnp.concatenate([real[:, half:], real[:, :half]], axis=1) * sign
        both = jnp.concatenate([real, imag], axis=0)
        product = jnp.dot(both, x_ref[i], preferred_element_type=jnp.float32)
        for part in range(2):
            for h in range(halves):
                cross[h, pl.ds(part * bin_count + f, rows, stride=stride), :] = product[
                    part * rows:(part + 1) * rows, h * 128:(h + 1) * 128
                ]

    @pl.when(step == pl.num_programs(0) - 1)
    def _():
        lags = out_ref.shape[1]

        def one_row(k, carry):
            at = pl.multiple_of(k * stride, 8)
            block = jnp.concatenate(
                [cross[h, pl.ds(at, 2 * bin_count), :].astype(jnp.bfloat16) for h in range(halves)], axis=1
            )
            lagged = jnp.dot(table_ref[...], block, preferred_element_type=jnp.float32)
            out_ref[k] = lagged[:lags].astype(jnp.bfloat16)
            return carry

        lax.fori_loop(0, rows, one_row, 0, unroll=4)


def correlate(sign, table, sources, x, bins):
    _, rows, depth = sources.shape
    bin_count, _, width = x.shape
    stride = -(-2 * bin_count // 8) * 8
    return pl.pallas_call(
        functools.partial(correlate_kernel, stride, bin_count),
        grid=(bin_count // bins,),
        in_specs=[
            pl.BlockSpec(sign.shape, lambda i: (0, 0)),
            pl.BlockSpec(table.shape, lambda i: (0, 0)),
            pl.BlockSpec((bins, rows, depth), lambda i: (i, 0, 0)),
            pl.BlockSpec((bins, depth, width), lambda i: (i, 0, 0)),
        ],
        out_specs=pl.BlockSpec((rows, LAGS, width), lambda i: (0, 0, 0)),
        out_shape=jax.ShapeDtypeStruct((rows, LAGS, width), jnp.bfloat16),
        scratch_shapes=[pltpu.VMEM((width // 128, rows * stride, 128), jnp.float32)],
        compiler_params=pltpu.CompilerParams(vmem_limit_bytes=48 * MIB),
        cost_estimate=pl.CostEstimate(
            flops=2 * bin_count * 2 * rows * depth * width + 2 * 2 * bin_count * rows * LAGS * width,
            bytes_accessed=2 * bin_count * depth * (width + rows) + 2 * rows * LAGS * width,
            transcendentals=0,
        ),
    )(sign, table, sources, x)


def add(a, b):
    return (a.astype(jnp.float32) + b.astype(jnp.float32)).astype(jnp.bfloat16)


def swap(x, axis, bit):
    return lax.ppermute(x, axis, [(i, i ^ (1 << bit)) for i in range(lax.axis_size(axis))])


def halve(current, axis, bits):
    for bit in bits:
        side = (lax.axis_index(axis) >> bit) & 1
        length = current.shape[0] // 2
        sent = lax.dynamic_slice_in_dim(current, (1 - side) * length, length, 0)
        kept = lax.dynamic_slice_in_dim(current, side * length, length, 0)
        current = add(kept, swap(sent, axis, bit))
    return current


def double(current, axis, bits):
    for bit in reversed(bits):
        side = (lax.axis_index(axis) >> bit) & 1
        other = swap(current, axis, bit)
        low, high = jnp.where(side == 0, current, other), jnp.where(side == 0, other, current)
        current = jnp.concatenate([low, high], axis=0)
    return current


def sum_of_chan(mine, after):
    bit_count = (lax.axis_size("chan") - 1).bit_length()
    length = mine.shape[0] // 2
    orders = [list(range(1, bit_count)), list(range(1, bit_count))[::-1]]
    parts = [halve(mine[:length], "chan", [0]), halve(mine[length:], "chan", [0])]
    if after is not None:
        parts, after = lax.optimization_barrier((parts, after))
    parts = [halve(part, "chan", order) for part, order in zip(parts, orders)]
    parts = [double(part, "chan", order) for part, order in zip(parts, orders)]
    return parts, after


def finish(parts):
    return jnp.concatenate([double(part, "chan", [0]) for part in parts], axis=0)


def chain_scatter(parts, axis):
    n, at = lax.axis_size(axis), lax.axis_index(axis)
    total = None
    from_left = from_right = None
    for t in range(n - 1):
        to_right = lax.dynamic_index_in_dim(parts, jnp.clip(n - 1 - t + at, 0, n - 1), 0, keepdims=False)
        to_left = lax.dynamic_index_in_dim(parts, jnp.clip(t + at - (n - 1), 0, n - 1), 0, keepdims=False)
        if t:
            to_right, to_left = add(to_right, from_left), add(to_left, from_right)
        from_left = lax.ppermute(to_right, axis, [(i, i + 1) for i in range(t + 1)])
        from_right = lax.ppermute(to_left, axis, [(n - 1 - i, n - 2 - i) for i in range(t + 1)])
    own = lax.dynamic_index_in_dim(parts, at, 0, keepdims=False).astype(jnp.float32)
    total = own + from_left.astype(jnp.float32) + from_right.astype(jnp.float32)
    return total.astype(jnp.bfloat16)


def body(spectra, src_blocks, valid):
    seg_count, _, bin_count, width = spectra.shape
    tm_count = lax.axis_size("tm")
    chan_index = lax.axis_index("chan")
    depth = 2 * seg_count
    sources_all = 2 * SRC_BLK
    per_dev = sources_all // tm_count

    keep = jnp.tile(valid.astype(jnp.float32), 2)[None, :]
    sign = np.where(np.arange(depth) < seg_count, -1.0, 1.0).astype(ml_dtypes.bfloat16)[None, :]
    table = lag_table(bin_count, LAGS, seg_count * tm_count)
    table = table.transpose(1, 0, 2).reshape(LAGS, 2 * bin_count)
    table = np.pad(table, ((0, -LAGS % 16), (0, 0)))
    sign, table = jnp.asarray(sign), jnp.asarray(table)

    def pick_of(first, rows):
        order = np.arange(sources_all, dtype=np.int32).reshape(tm_count, per_dev)
        order = order[:, first:first + rows].reshape(-1)
        channel = src_blocks[order // SRC_BLK] * SRC_BLK + order % SRC_BLK - chan_index * width
        return (channel[:, None] == jnp.arange(width, dtype=jnp.int32)[None, :]).astype(jnp.bfloat16)

    x = spectra.transpose(2, 1, 0, 3).reshape(bin_count, depth, width)
    summed = []
    after = None
    first = 0
    for rows in ROWS:
        mine = pick_sources(pick_of(first, rows), keep, x, 25)
        parts, after = sum_of_chan(mine, after)
        if after is not None:
            summed.append(after)
        after = parts
        first += rows
    summed.append(after)
    outs = []
    for rows, parts in zip(ROWS, summed):
        partial_value = correlate(sign, table, finish(parts), x, 25)
        outs.append(chain_scatter(partial_value.reshape(tm_count, rows, LAGS, width), "tm"))
    return jnp.concatenate(outs, axis=0)


def solution(mesh):
    placed = (P("tm", None, None, "chan"), P(), P("tm"))
    return jax.shard_map(
        body, mesh=mesh, in_specs=placed, out_specs=P("tm", None, "chan"), check_vma=False
    )
```

```python
import functools

import jax
import jax.numpy as jnp
import ml_dtypes
import numpy as np
from jax import lax
from jax.experimental import pallas as pl
from jax.experimental.pallas import tpu as pltpu
from jax.sharding import PartitionSpec as P

LAGS = 101
SRC_BLK = 64
ROWS = (8, 12, 12)
AHEAD = (3, 2)
PAD = 256
MIB = 1024 * 1024


def lag_table(bin_count, lag_count, segment_total):
    bins_idx = np.arange(bin_count) + 1
    lag_steps = np.arange(lag_count) - (lag_count - 1) // 2
    phase_int = lag_steps[:, None] * bins_idx[None, :] % (2 * bin_count)
    phase = phase_int * (2.0 * np.pi / (2.0 * bin_count))
    scale = 1.0 / np.sqrt(float(segment_total * bin_count))
    return np.stack([np.cos(phase) * scale, -np.sin(phase) * scale]).astype(ml_dtypes.bfloat16)


def pick_kernel(pick_ref, keep_ref, x_ref, out_ref):
    for f in range(out_ref.shape[0]):
        picked = lax.dot_general(
            pick_ref[...], x_ref[f], (((1,), (1,)), ((), ())), preferred_element_type=jnp.float32
        )
        out_ref[f] = (picked * keep_ref[...]).astype(jnp.bfloat16)


def pick_sources(pick, keep, x, bins):
    bin_count, depth, width = x.shape
    rows = pick.shape[0]
    return pl.pallas_call(
        pick_kernel,
        grid=(bin_count // bins,),
        in_specs=[
            pl.BlockSpec(pick.shape, lambda i: (0, 0)),
            pl.BlockSpec(keep.shape, lambda i: (0, 0)),
            pl.BlockSpec((bins, depth, width), lambda i: (i, 0, 0)),
        ],
        out_specs=pl.BlockSpec((bins, rows, depth), lambda i: (i, 0, 0)),
        out_shape=jax.ShapeDtypeStruct((-(-bin_count // PAD) * PAD, rows, depth), jnp.bfloat16),
        compiler_params=pltpu.CompilerParams(vmem_limit_bytes=52 * MIB),
        cost_estimate=pl.CostEstimate(
            flops=2 * bin_count * rows * width * depth,
            bytes_accessed=2 * bin_count * depth * (width + rows),
            transcendentals=0,
        ),
    )(pick, keep, x)


def correlate_kernel(stride, bin_count, sign_ref, table_ref, source_ref, x_ref, out_ref, cross):
    bins, rows, depth = source_ref.shape
    width = x_ref.shape[2]
    halves = width // 128
    step = pl.program_id(0)
    sign = sign_ref[...]
    for i in range(bins):
        f = step * bins + i
        real = source_ref[i]
        half = depth // 2
        imag = jnp.concatenate([real[:, half:], real[:, :half]], axis=1) * sign
        both = jnp.concatenate([real, imag], axis=0)
        product = jnp.dot(both, x_ref[i], preferred_element_type=jnp.float32)
        for part in range(2):
            for h in range(halves):
                cross[h, pl.ds(part * bin_count + f, rows, stride=stride), :] = product[
                    part * rows:(part + 1) * rows, h * 128:(h + 1) * 128
                ]

    @pl.when(step == pl.num_programs(0) - 1)
    def _():
        lags = out_ref.shape[1]

        def one_row(k, carry):
            at = pl.multiple_of(k * stride, 8)
            block = jnp.concatenate(
                [cross[h, pl.ds(at, 2 * bin_count), :].astype(jnp.bfloat16) for h in range(halves)], axis=1
            )
            lagged = jnp.dot(table_ref[...], block, preferred_element_type=jnp.float32)
            out_ref[k] = lagged[:lags].astype(jnp.bfloat16)
            return carry

        lax.fori_loop(0, rows, one_row, 0, unroll=4)


def correlate(sign, table, sources, x, bins):
    _, rows, depth = sources.shape
    bin_count, _, width = x.shape
    stride = -(-2 * bin_count // 8) * 8
    return pl.pallas_call(
        functools.partial(correlate_kernel, stride, bin_count),
        grid=(bin_count // bins,),
        in_specs=[
            pl.BlockSpec(sign.shape, lambda i: (0, 0)),
            pl.BlockSpec(table.shape, lambda i: (0, 0)),
            pl.BlockSpec((bins, rows, depth), lambda i: (i, 0, 0)),
            pl.BlockSpec((bins, depth, width), lambda i: (i, 0, 0)),
        ],
        out_specs=pl.BlockSpec((rows, LAGS, width), lambda i: (0, 0, 0)),
        out_shape=jax.ShapeDtypeStruct((rows, LAGS, width), jnp.bfloat16),
        scratch_shapes=[pltpu.VMEM((width // 128, rows * stride, 128), jnp.float32)],
        compiler_params=pltpu.CompilerParams(vmem_limit_bytes=52 * MIB),
        cost_estimate=pl.CostEstimate(
            flops=2 * bin_count * 2 * rows * depth * width + 2 * 2 * bin_count * rows * LAGS * width,
            bytes_accessed=2 * bin_count * depth * (width + rows) + 2 * rows * LAGS * width,
            transcendentals=0,
        ),
    )(sign, table, sources, x)


def add(a, b):
    return (a.astype(jnp.float32) + b.astype(jnp.float32)).astype(jnp.bfloat16)


def swap(x, axis, bit):
    return lax.ppermute(x, axis, [(i, i ^ (1 << bit)) for i in range(lax.axis_size(axis))])


def halve(current, axis, bits):
    for bit in bits:
        side = (lax.axis_index(axis) >> bit) & 1
        length = current.shape[0] // 2
        sent = lax.dynamic_slice_in_dim(current, (1 - side) * length, length, 0)
        kept = lax.dynamic_slice_in_dim(current, side * length, length, 0)
        current = add(kept, swap(sent, axis, bit))
    return current


def double(current, axis, bits):
    for bit in reversed(bits):
        side = (lax.axis_index(axis) >> bit) & 1
        other = swap(current, axis, bit)
        low, high = jnp.where(side == 0, current, other), jnp.where(side == 0, other, current)
        current = jnp.concatenate([low, high], axis=0)
    return current


def orders():
    rest = list(range(1, (lax.axis_size("chan") - 1).bit_length()))
    return rest, rest[::-1]


def begin(mine):
    length = mine.shape[0] // 2
    return [halve(mine[:length], "chan", [0]), halve(mine[length:], "chan", [0])]


def halve_rest(parts):
    return [halve(part, "chan", order) for part, order in zip(parts, orders())]


def double_rest(parts):
    return [double(part, "chan", order) for part, order in zip(parts, orders())]


def finish(parts):
    return jnp.concatenate([double(part, "chan", [0]) for part in parts], axis=0)


def take(parts, at):
    return lax.dynamic_index_in_dim(parts, jnp.clip(at, 0, parts.shape[0] - 1), 0, keepdims=False)


def chain_steps(parts, state, axis, first, last):
    n, at = lax.axis_size(axis), lax.axis_index(axis)
    for t in range(first, last):
        to_right, to_left = take(parts, n - 1 - t + at), take(parts, t + at - (n - 1))
        if t:
            to_right, to_left = add(to_right, state[0]), add(to_left, state[1])
        state = (
            lax.ppermute(to_right, axis, [(i, i + 1) for i in range(t + 1)]),
            lax.ppermute(to_left, axis, [(n - 1 - i, n - 2 - i) for i in range(t + 1)]),
        )
    return state


def chain_end(parts, state, axis):
    own = take(parts, lax.axis_index(axis)).astype(jnp.float32)
    return (own + state[0].astype(jnp.float32) + state[1].astype(jnp.float32)).astype(jnp.bfloat16)


def body(spectra, src_blocks, valid):
    seg_count, _, bin_count, width = spectra.shape
    tm_count = lax.axis_size("tm")
    chan_index = lax.axis_index("chan")
    depth = 2 * seg_count
    sources_all = 2 * SRC_BLK
    per_dev = sources_all // tm_count

    keep = jnp.tile(valid.astype(jnp.float32), 2)[None, :]
    sign = np.where(np.arange(depth) < seg_count, -1.0, 1.0).astype(ml_dtypes.bfloat16)[None, :]
    table = lag_table(bin_count, LAGS, seg_count * tm_count)
    table = table.transpose(1, 0, 2).reshape(LAGS, 2 * bin_count)
    table = np.pad(table, ((0, -LAGS % 16), (0, 0)))
    sign, table = jnp.asarray(sign), jnp.asarray(table)

    def pick_of(first, rows):
        order = np.arange(sources_all, dtype=np.int32).reshape(tm_count, per_dev)
        order = order[:, first:first + rows].reshape(-1)
        channel = src_blocks[order // SRC_BLK] * SRC_BLK + order % SRC_BLK - chan_index * width
        return (channel[:, None] == jnp.arange(width, dtype=jnp.int32)[None, :]).astype(jnp.bfloat16)

    x = spectra.transpose(2, 1, 0, 3).reshape(bin_count, depth, width)
    steps = tm_count - 1
    outs = []
    done = chain = None
    first = 0

    def correlograms(done, rows):
        return correlate(sign, table, done, x, 25).reshape(tm_count, rows, LAGS, width)

    coming = begin(pick_sources(pick_of(0, ROWS[0]), keep, x, 25))
    for at, rows in enumerate(ROWS):
        parts = coming
        if at:
            parts, done = lax.optimization_barrier((parts, done))
        first += rows
        if at + 1 < len(ROWS):
            parts, keep = lax.optimization_barrier((parts, keep))
            coming = begin(pick_sources(pick_of(first, ROWS[at + 1]), keep, x, 25))
        parts = halve_rest(parts)
        if at:
            source = finish(done)
            if chain is not None:
                ahead = min(AHEAD[at - 2], steps)
                state = chain_steps(chain, None, "tm", 0, ahead)
                source, state = lax.optimization_barrier((source, state))
                state = chain_steps(chain, state, "tm", ahead, steps)
                outs.append(chain_end(chain, state, "tm"))
            chain = correlograms(source, ROWS[at - 1])
            parts, chain = lax.optimization_barrier((parts, chain))
        done = double_rest(parts)
    source = finish(done)
    ahead = min(AHEAD[-1], steps)
    state = chain_steps(chain, None, "tm", 0, ahead)
    source, state = lax.optimization_barrier((source, state))
    state = chain_steps(chain, state, "tm", ahead, steps)
    outs.append(chain_end(chain, state, "tm"))
    chain = correlograms(source, ROWS[-1])
    outs.append(chain_end(chain, chain_steps(chain, None, "tm", 0, steps), "tm"))
    return jnp.concatenate(outs, axis=0)


def solution(mesh):
    placed = (P("tm", None, None, "chan"), P(), P("tm"))
    return jax.shard_map(
        body, mesh=mesh, in_specs=placed, out_specs=P("tm", None, "chan"), check_vma=False
    )
```

```python
import functools

import jax
import jax.numpy as jnp
import ml_dtypes
import numpy as np
from jax import lax
from jax.experimental import pallas as pl
from jax.experimental.pallas import tpu as pltpu
from jax.sharding import PartitionSpec as P

LAGS = 101
SRC_BLK = 64
ROWS = (20, 12)
AHEAD = (2,)
PAD = 256
MIB = 1024 * 1024


def lag_table(bin_count, lag_count, segment_total):
    bins_idx = np.arange(bin_count) + 1
    lag_steps = np.arange(lag_count) - (lag_count - 1) // 2
    phase_int = lag_steps[:, None] * bins_idx[None, :] % (2 * bin_count)
    phase = phase_int * (2.0 * np.pi / (2.0 * bin_count))
    scale = 1.0 / np.sqrt(float(segment_total * bin_count))
    return np.stack([np.cos(phase) * scale, -np.sin(phase) * scale]).astype(ml_dtypes.bfloat16)


def pick_kernel(pick_ref, keep_ref, x_ref, out_ref):
    for f in range(out_ref.shape[0]):
        picked = lax.dot_general(
            pick_ref[...], x_ref[f], (((1,), (1,)), ((), ())), preferred_element_type=jnp.float32
        )
        out_ref[f] = (picked * keep_ref[...]).astype(jnp.bfloat16)


def pick_sources(pick, keep, x, bins):
    bin_count, depth, width = x.shape
    rows = pick.shape[0]
    return pl.pallas_call(
        pick_kernel,
        grid=(bin_count // bins,),
        in_specs=[
            pl.BlockSpec(pick.shape, lambda i: (0, 0)),
            pl.BlockSpec(keep.shape, lambda i: (0, 0)),
            pl.BlockSpec((bins, depth, width), lambda i: (i, 0, 0)),
        ],
        out_specs=pl.BlockSpec((bins, rows, depth), lambda i: (i, 0, 0)),
        out_shape=jax.ShapeDtypeStruct((-(-bin_count // PAD) * PAD, rows, depth), jnp.bfloat16),
        compiler_params=pltpu.CompilerParams(vmem_limit_bytes=52 * MIB),
        cost_estimate=pl.CostEstimate(
            flops=2 * bin_count * rows * width * depth,
            bytes_accessed=2 * bin_count * depth * (width + rows),
            transcendentals=0,
        ),
    )(pick, keep, x)


def correlate_kernel(stride, bin_count, sign_ref, table_ref, source_ref, x_ref, out_ref, cross):
    bins, rows, depth = source_ref.shape
    width = x_ref.shape[2]
    halves = width // 128
    step = pl.program_id(0)
    sign = sign_ref[...]
    for i in range(bins):
        f = step * bins + i
        real = source_ref[i]
        half = depth // 2
        imag = jnp.concatenate([real[:, half:], real[:, :half]], axis=1) * sign
        both = jnp.concatenate([real, imag], axis=0)
        product = jnp.dot(both, x_ref[i], preferred_element_type=jnp.float32)
        for part in range(2):
            for h in range(halves):
                cross[h, pl.ds(part * bin_count + f, rows, stride=stride), :] = product[
                    part * rows:(part + 1) * rows, h * 128:(h + 1) * 128
                ]

    @pl.when(step == pl.num_programs(0) - 1)
    def _():
        lags = out_ref.shape[1]

        def one_row(k, carry):
            at = pl.multiple_of(k * stride, 8)
            block = jnp.concatenate(
                [cross[h, pl.ds(at, 2 * bin_count), :].astype(jnp.bfloat16) for h in range(halves)], axis=1
            )
            lagged = jnp.dot(table_ref[...], block, preferred_element_type=jnp.float32)
            out_ref[k] = lagged[:lags].astype(jnp.bfloat16)
            return carry

        lax.fori_loop(0, rows, one_row, 0, unroll=4)


def correlate(sign, table, sources, x, bins):
    _, rows, depth = sources.shape
    bin_count, _, width = x.shape
    stride = -(-2 * bin_count // 8) * 8
    return pl.pallas_call(
        functools.partial(correlate_kernel, stride, bin_count),
        grid=(bin_count // bins,),
        in_specs=[
            pl.BlockSpec(sign.shape, lambda i: (0, 0)),
            pl.BlockSpec(table.shape, lambda i: (0, 0)),
            pl.BlockSpec((bins, rows, depth), lambda i: (i, 0, 0)),
            pl.BlockSpec((bins, depth, width), lambda i: (i, 0, 0)),
        ],
        out_specs=pl.BlockSpec((rows, LAGS, width), lambda i: (0, 0, 0)),
        out_shape=jax.ShapeDtypeStruct((rows, LAGS, width), jnp.bfloat16),
        scratch_shapes=[pltpu.VMEM((width // 128, rows * stride, 128), jnp.float32)],
        compiler_params=pltpu.CompilerParams(vmem_limit_bytes=58 * MIB),
        cost_estimate=pl.CostEstimate(
            flops=2 * bin_count * 2 * rows * depth * width + 2 * 2 * bin_count * rows * LAGS * width,
            bytes_accessed=2 * bin_count * depth * (width + rows) + 2 * rows * LAGS * width,
            transcendentals=0,
        ),
    )(sign, table, sources, x)


def add(a, b):
    return (a.astype(jnp.float32) + b.astype(jnp.float32)).astype(jnp.bfloat16)


def swap(x, axis, bit):
    return lax.ppermute(x, axis, [(i, i ^ (1 << bit)) for i in range(lax.axis_size(axis))])


def halve(current, axis, bits):
    for bit in bits:
        side = (lax.axis_index(axis) >> bit) & 1
        length = current.shape[0] // 2
        sent = lax.dynamic_slice_in_dim(current, (1 - side) * length, length, 0)
        kept = lax.dynamic_slice_in_dim(current, side * length, length, 0)
        current = add(kept, swap(sent, axis, bit))
    return current


def double(current, axis, bits):
    for bit in reversed(bits):
        side = (lax.axis_index(axis) >> bit) & 1
        other = swap(current, axis, bit)
        low, high = jnp.where(side == 0, current, other), jnp.where(side == 0, other, current)
        current = jnp.concatenate([low, high], axis=0)
    return current


def orders():
    rest = list(range(1, (lax.axis_size("chan") - 1).bit_length()))
    return rest, rest[::-1]


def begin(mine):
    length = mine.shape[0] // 2
    return [halve(mine[:length], "chan", [0]), halve(mine[length:], "chan", [0])]


def halve_rest(parts):
    return [halve(part, "chan", order) for part, order in zip(parts, orders())]


def double_rest(parts):
    return [double(part, "chan", order) for part, order in zip(parts, orders())]


def finish(parts):
    return jnp.concatenate([double(part, "chan", [0]) for part in parts], axis=0)


def take(parts, at):
    return lax.dynamic_index_in_dim(parts, jnp.clip(at, 0, parts.shape[0] - 1), 0, keepdims=False)


def chain_steps(parts, state, axis, first, last):
    n, at = lax.axis_size(axis), lax.axis_index(axis)
    for t in range(first, last):
        to_right, to_left = take(parts, n - 1 - t + at), take(parts, t + at - (n - 1))
        if t:
            to_right, to_left = add(to_right, state[0]), add(to_left, state[1])
        state = (
            lax.ppermute(to_right, axis, [(i, i + 1) for i in range(t + 1)]),
            lax.ppermute(to_left, axis, [(n - 1 - i, n - 2 - i) for i in range(t + 1)]),
        )
    return state


def chain_end(parts, state, axis):
    own = take(parts, lax.axis_index(axis)).astype(jnp.float32)
    return (own + state[0].astype(jnp.float32) + state[1].astype(jnp.float32)).astype(jnp.bfloat16)


def body(spectra, src_blocks, valid):
    seg_count, _, bin_count, width = spectra.shape
    tm_count = lax.axis_size("tm")
    chan_index = lax.axis_index("chan")
    depth = 2 * seg_count
    sources_all = 2 * SRC_BLK
    per_dev = sources_all // tm_count

    keep = jnp.tile(valid.astype(jnp.float32), 2)[None, :]
    sign = np.where(np.arange(depth) < seg_count, -1.0, 1.0).astype(ml_dtypes.bfloat16)[None, :]
    table = lag_table(bin_count, LAGS, seg_count * tm_count)
    table = table.transpose(1, 0, 2).reshape(LAGS, 2 * bin_count)
    table = np.pad(table, ((0, -LAGS % 16), (0, 0)))
    sign, table = jnp.asarray(sign), jnp.asarray(table)

    def pick_of(first, rows):
        order = np.arange(sources_all, dtype=np.int32).reshape(tm_count, per_dev)
        order = order[:, first:first + rows].reshape(-1)
        channel = src_blocks[order // SRC_BLK] * SRC_BLK + order % SRC_BLK - chan_index * width
        return (channel[:, None] == jnp.arange(width, dtype=jnp.int32)[None, :]).astype(jnp.bfloat16)

    x = spectra.transpose(2, 1, 0, 3).reshape(bin_count, depth, width)
    steps = tm_count - 1
    outs = []
    done = chain = None
    first = 0

    def correlograms(done, rows):
        return correlate(sign, table, done, x, 25).reshape(tm_count, rows, LAGS, width)

    coming = begin(pick_sources(pick_of(0, ROWS[0]), keep, x, 25))
    for at, rows in enumerate(ROWS):
        parts = coming
        if at:
            parts, done = lax.optimization_barrier((parts, done))
        first += rows
        if at + 1 < len(ROWS):
            parts, keep = lax.optimization_barrier((parts, keep))
            coming = begin(pick_sources(pick_of(first, ROWS[at + 1]), keep, x, 25))
        parts = halve_rest(parts)
        if at:
            source = finish(done)
            if chain is not None:
                ahead = min(AHEAD[at - 2], steps)
                state = chain_steps(chain, None, "tm", 0, ahead)
                source, state = lax.optimization_barrier((source, state))
                state = chain_steps(chain, state, "tm", ahead, steps)
                outs.append(chain_end(chain, state, "tm"))
            chain = correlograms(source, ROWS[at - 1])
            parts, chain = lax.optimization_barrier((parts, chain))
        done = double_rest(parts)
    source = finish(done)
    ahead = min(AHEAD[-1], steps)
    state = chain_steps(chain, None, "tm", 0, ahead)
    source, state = lax.optimization_barrier((source, state))
    state = chain_steps(chain, state, "tm", ahead, steps)
    outs.append(chain_end(chain, state, "tm"))
    chain = correlograms(source, ROWS[-1])
    outs.append(chain_end(chain, chain_steps(chain, None, "tm", 0, steps), "tm"))
    return jnp.concatenate(outs, axis=0)


def solution(mesh):
    placed = (P("tm", None, None, "chan"), P(), P("tm"))
    return jax.shard_map(
        body, mesh=mesh, in_specs=placed, out_specs=P("tm", None, "chan"), check_vma=False
    )
```

```python
import functools

import jax
import jax.numpy as jnp
import ml_dtypes
import numpy as np
from jax import lax
from jax.experimental import pallas as pl
from jax.experimental.pallas import tpu as pltpu
from jax.sharding import PartitionSpec as P

LAGS = 101
SRC_BLK = 64
ROWS = (16, 16)
AHEAD = (2,)
PAD = 256
MIB = 1024 * 1024


def lag_table(bin_count, lag_count, segment_total):
    bins_idx = np.arange(bin_count) + 1
    lag_steps = np.arange(lag_count) - (lag_count - 1) // 2
    phase_int = lag_steps[:, None] * bins_idx[None, :] % (2 * bin_count)
    phase = phase_int * (2.0 * np.pi / (2.0 * bin_count))
    scale = 1.0 / np.sqrt(float(segment_total * bin_count))
    return np.stack([np.cos(phase) * scale, -np.sin(phase) * scale]).astype(ml_dtypes.bfloat16)


def pick_kernel(pick_ref, keep_ref, x_ref, out_ref):
    for f in range(out_ref.shape[0]):
        picked = lax.dot_general(
            pick_ref[...], x_ref[f], (((1,), (1,)), ((), ())), preferred_element_type=jnp.float32
        )
        out_ref[f] = (picked * keep_ref[...]).astype(jnp.bfloat16)


def pick_sources(pick, keep, x, bins):
    bin_count, depth, width = x.shape
    rows = pick.shape[0]
    return pl.pallas_call(
        pick_kernel,
        grid=(bin_count // bins,),
        in_specs=[
            pl.BlockSpec(pick.shape, lambda i: (0, 0)),
            pl.BlockSpec(keep.shape, lambda i: (0, 0)),
            pl.BlockSpec((bins, depth, width), lambda i: (i, 0, 0)),
        ],
        out_specs=pl.BlockSpec((bins, rows, depth), lambda i: (i, 0, 0)),
        out_shape=jax.ShapeDtypeStruct((-(-bin_count // PAD) * PAD, rows, depth), jnp.bfloat16),
        compiler_params=pltpu.CompilerParams(vmem_limit_bytes=52 * MIB),
        cost_estimate=pl.CostEstimate(
            flops=2 * bin_count * rows * width * depth,
            bytes_accessed=2 * bin_count * depth * (width + rows),
            transcendentals=0,
        ),
    )(pick, keep, x)


def correlate_kernel(stride, bin_count, sign_ref, table_ref, source_ref, x_ref, out_ref, cross):
    bins, rows, depth = source_ref.shape
    width = x_ref.shape[2]
    halves = width // 128
    step = pl.program_id(0)
    sign = sign_ref[...]
    for i in range(bins):
        f = step * bins + i
        real = source_ref[i]
        half = depth // 2
        imag = jnp.concatenate([real[:, half:], real[:, :half]], axis=1) * sign
        both = jnp.concatenate([real, imag], axis=0)
        product = jnp.dot(both, x_ref[i], preferred_element_type=jnp.float32)
        for part in range(2):
            for h in range(halves):
                cross[h, pl.ds(part * bin_count + f, rows, stride=stride), :] = product[
                    part * rows:(part + 1) * rows, h * 128:(h + 1) * 128
                ]

    @pl.when(step == pl.num_programs(0) - 1)
    def _():
        lags = out_ref.shape[1]

        def one_row(k, carry):
            at = pl.multiple_of(k * stride, 8)
            block = jnp.concatenate(
                [cross[h, pl.ds(at, 2 * bin_count), :].astype(jnp.bfloat16) for h in range(halves)], axis=1
            )
            lagged = jnp.dot(table_ref[...], block, preferred_element_type=jnp.float32)
            out_ref[k] = lagged[:lags].astype(jnp.bfloat16)
            return carry

        lax.fori_loop(0, rows, one_row, 0, unroll=4)


def correlate(sign, table, sources, x, bins):
    _, rows, depth = sources.shape
    bin_count, _, width = x.shape
    stride = -(-2 * bin_count // 8) * 8
    return pl.pallas_call(
        functools.partial(correlate_kernel, stride, bin_count),
        grid=(bin_count // bins,),
        in_specs=[
            pl.BlockSpec(sign.shape, lambda i: (0, 0)),
            pl.BlockSpec(table.shape, lambda i: (0, 0)),
            pl.BlockSpec((bins, rows, depth), lambda i: (i, 0, 0)),
            pl.BlockSpec((bins, depth, width), lambda i: (i, 0, 0)),
        ],
        out_specs=pl.BlockSpec((rows, LAGS, width), lambda i: (0, 0, 0)),
        out_shape=jax.ShapeDtypeStruct((rows, LAGS, width), jnp.bfloat16),
        scratch_shapes=[pltpu.VMEM((width // 128, rows * stride, 128), jnp.float32)],
        compiler_params=pltpu.CompilerParams(vmem_limit_bytes=58 * MIB),
        cost_estimate=pl.CostEstimate(
            flops=2 * bin_count * 2 * rows * depth * width + 2 * 2 * bin_count * rows * LAGS * width,
            bytes_accessed=2 * bin_count * depth * (width + rows) + 2 * rows * LAGS * width,
            transcendentals=0,
        ),
    )(sign, table, sources, x)


def add(a, b):
    return (a.astype(jnp.float32) + b.astype(jnp.float32)).astype(jnp.bfloat16)


def swap(x, axis, bit):
    return lax.ppermute(x, axis, [(i, i ^ (1 << bit)) for i in range(lax.axis_size(axis))])


def halve(current, axis, bits):
    for bit in bits:
        side = (lax.axis_index(axis) >> bit) & 1
        length = current.shape[0] // 2
        sent = lax.dynamic_slice_in_dim(current, (1 - side) * length, length, 0)
        kept = lax.dynamic_slice_in_dim(current, side * length, length, 0)
        current = add(kept, swap(sent, axis, bit))
    return current


def double(current, axis, bits):
    for bit in reversed(bits):
        side = (lax.axis_index(axis) >> bit) & 1
        other = swap(current, axis, bit)
        low, high = jnp.where(side == 0, current, other), jnp.where(side == 0, other, current)
        current = jnp.concatenate([low, high], axis=0)
    return current


def orders():
    rest = list(range(1, (lax.axis_size("chan") - 1).bit_length()))
    return rest, rest[::-1]


def begin(mine):
    length = mine.shape[0] // 2
    return [halve(mine[:length], "chan", [0]), halve(mine[length:], "chan", [0])]


def halve_rest(parts):
    return [halve(part, "chan", order) for part, order in zip(parts, orders())]


def double_rest(parts):
    return [double(part, "chan", order) for part, order in zip(parts, orders())]


def finish(parts):
    return jnp.concatenate([double(part, "chan", [0]) for part in parts], axis=0)


def take(parts, at):
    return lax.dynamic_index_in_dim(parts, jnp.clip(at, 0, parts.shape[0] - 1), 0, keepdims=False)


def chain_steps(parts, state, axis, first, last):
    n, at = lax.axis_size(axis), lax.axis_index(axis)
    for t in range(first, last):
        to_right, to_left = take(parts, n - 1 - t + at), take(parts, t + at - (n - 1))
        if t:
            to_right, to_left = add(to_right, state[0]), add(to_left, state[1])
        state = (
            lax.ppermute(to_right, axis, [(i, i + 1) for i in range(t + 1)]),
            lax.ppermute(to_left, axis, [(n - 1 - i, n - 2 - i) for i in range(t + 1)]),
        )
    return state


def chain_end(parts, state, axis):
    own = take(parts, lax.axis_index(axis)).astype(jnp.float32)
    return (own + state[0].astype(jnp.float32) + state[1].astype(jnp.float32)).astype(jnp.bfloat16)


def body(spectra, src_blocks, valid):
    seg_count, _, bin_count, width = spectra.shape
    tm_count = lax.axis_size("tm")
    chan_index = lax.axis_index("chan")
    depth = 2 * seg_count
    sources_all = 2 * SRC_BLK
    per_dev = sources_all // tm_count

    keep = jnp.tile(valid.astype(jnp.float32), 2)[None, :]
    sign = np.where(np.arange(depth) < seg_count, -1.0, 1.0).astype(ml_dtypes.bfloat16)[None, :]
    table = lag_table(bin_count, LAGS, seg_count * tm_count)
    table = table.transpose(1, 0, 2).reshape(LAGS, 2 * bin_count)
    table = np.pad(table, ((0, -LAGS % 16), (0, 0)))
    sign, table = jnp.asarray(sign), jnp.asarray(table)

    def pick_of(first, rows):
        order = np.arange(sources_all, dtype=np.int32).reshape(tm_count, per_dev)
        order = order[:, first:first + rows].reshape(-1)
        channel = src_blocks[order // SRC_BLK] * SRC_BLK + order % SRC_BLK - chan_index * width
        return (channel[:, None] == jnp.arange(width, dtype=jnp.int32)[None, :]).astype(jnp.bfloat16)

    x = spectra.transpose(2, 1, 0, 3).reshape(bin_count, depth, width)
    steps = tm_count - 1
    outs = []
    done = chain = None
    first = 0

    def correlograms(done, rows):
        return correlate(sign, table, done, x, 25).reshape(tm_count, rows, LAGS, width)

    coming = begin(pick_sources(pick_of(0, ROWS[0]), keep, x, 25))
    for at, rows in enumerate(ROWS):
        parts = coming
        if at:
            parts, done = lax.optimization_barrier((parts, done))
        first += rows
        if at + 1 < len(ROWS):
            parts, keep = lax.optimization_barrier((parts, keep))
            coming = begin(pick_sources(pick_of(first, ROWS[at + 1]), keep, x, 25))
        if at:
            source = finish(done)
            if chain is not None:
                ahead = min(AHEAD[at - 2], steps)
                state = chain_steps(chain, None, "tm", 0, ahead)
                source, state = lax.optimization_barrier((source, state))
                state = chain_steps(chain, state, "tm", ahead, steps)
                outs.append(chain_end(chain, state, "tm"))
            chain = correlograms(source, ROWS[at - 1])
            parts, chain = lax.optimization_barrier((parts, chain))
        done = double_rest(halve_rest(parts))
    source = finish(done)
    ahead = min(AHEAD[-1], steps)
    state = chain_steps(chain, None, "tm", 0, ahead)
    source, state = lax.optimization_barrier((source, state))
    state = chain_steps(chain, state, "tm", ahead, steps)
    outs.append(chain_end(chain, state, "tm"))
    chain = correlograms(source, ROWS[-1])
    outs.append(chain_end(chain, chain_steps(chain, None, "tm", 0, steps), "tm"))
    return jnp.concatenate(outs, axis=0)


def solution(mesh):
    placed = (P("tm", None, None, "chan"), P(), P("tm"))
    return jax.shard_map(
        body, mesh=mesh, in_specs=placed, out_specs=P("tm", None, "chan"), check_vma=False
    )
```
